32 devices in a mesh: chan: 8 (over y, x, core), seq: 4 (over z).
Axes of the slice: x: 2, y: 2, z: 4, core: 2. Of those that a mesh axis runs over, the one named last changes fastest.
Arguments:
- queries: bfloat16 [8192, 1024], P('chan', 'seq'), may hold values from -6 to 6
- key_rows: bfloat16 [8192, 1024], P('chan', 'seq'), may hold values from -6 to 6
- value_rows: bfloat16 [8192, 1024], P('chan', 'seq'), may hold values from -6 to 6
- filters: float32 [8192, 1024], P('chan', 'seq'), may hold values from -0.1875 to 0.1875
- skip_gain: float32 [8192], P('chan'), may hold values from 0.1 to 1.9
- out_weight: bfloat16 [8192, 4096], P('chan'), may hold values from -0.09375 to 0.09375
Outputs:
- projected: float32 [4096, 1024], P('chan', 'seq')
The draws below stay inside these ranges and needn't reach their ends.
All inputs are finite; a program needn't handle non-finite values.
Results may differ from the reference program's by a relative error of at most 0.0029.
Values may be sent and summed in bfloat16 or wider, within the bound.
A program may use at most 128 MiB of HBM per device.

```python
import jax
import jax.numpy as jnp
from jax import lax

DM = 4096
CH = 8192
SEQ_LEN = 1024


def spiked(drawn, key, source, target, blocks, factor):
    def block_of(axis_at):
        return (jnp.arange(drawn.shape[axis_at]) // (drawn.shape[axis_at] // blocks)).reshape((-1,) + (1,) * (drawn.ndim - 1 - axis_at))

    first = jax.random.permutation(key, blocks)[block_of(target)]
    far = (block_of(target) + blocks // 2) % blocks
    return jnp.where((block_of(source) == first) | (block_of(source) == far), factor * drawn, drawn)


def steps_of(stream_key, dims, pieces, least, high):
    factor_of, own = 1.0, jax.random.fold_in(stream_key, 6)
    for axis_at, shards_of in pieces:
        steps = jnp.exp(jax.random.uniform(jax.random.fold_in(own, axis_at), (shards_of,), jnp.float32, least / len(pieces), high / len(pieces)))
        factor_of = factor_of * jnp.repeat(steps, dims[axis_at] // shards_of).reshape([-1 if axis == axis_at else 1 for axis in range(len(dims))])
    return factor_of


def gaussian(key, shape, scale, bound, pieces=(), kind=jnp.bfloat16):
    gain = steps_of(key, shape, pieces, -0.22, 0.18) if pieces else 1.0
    array = jax.random.normal(key, shape, jnp.float32) * scale * gain
    return jnp.minimum(jnp.maximum(array, -bound), bound).astype(kind)


def bell_draw_with(rng, dims, spread, limit, pieces, heavy, held_as=jnp.bfloat16):
    array = spread * jax.random.normal(rng, dims, jnp.float32)
    if pieces:
        array = array * steps_of(rng, dims, pieces, -0.22, 0.18)
    return jnp.clip(spiked(array, jax.random.fold_in(rng, 3), *heavy), -limit, limit).astype(held_as)


def setup_inputs(seed: int = 0) -> dict:
    streams_of = jax.random.split(jax.random.key(seed), 7)
    queries = gaussian(streams_of[0], (CH, SEQ_LEN), 1.0, 6.0, ((0, 8), (1, 4)))
    key_rows = gaussian(streams_of[1], (CH, SEQ_LEN), 1.0, 6.0, ((0, 8), (1, 4)))
    value_rows = gaussian(streams_of[2], (CH, SEQ_LEN), 1.0, 6.0, ((0, 8), (1, 4)))
    filters = gaussian(streams_of[3], (CH, SEQ_LEN), SEQ_LEN ** -0.5, 0.1875, ((0, 8), (1, 4)), jnp.float32)
    skip_gain = jnp.clip(1.0 + 0.18 * jax.random.normal(streams_of[4], (CH,), jnp.float32), 0.1, 1.9)
    out_weight = bell_draw_with(streams_of[5], (CH, DM), CH ** -0.5, 0.09375, ((0, 8),), (0, 1, 8, 2.0))
    return {"queries": queries, "key_rows": key_rows, "value_rows": value_rows, "filters": filters, "skip_gain": skip_gain, "out_weight": out_weight}


def reference(queries, key_rows, value_rows, filters, skip_gain, out_weight):
    gated = key_rows.astype(jnp.float32) * value_rows.astype(jnp.float32)
    length = gated.shape[1]
    spectrum = jnp.fft.rfft(gated, n=2 * length, axis=1) * jnp.fft.rfft(filters, n=2 * length, axis=1)
    conv = jnp.fft.irfft(spectrum, n=2 * length, axis=1)[:, :length]
    mixed = (queries.astype(jnp.float32) * (conv + skip_gain[:, None] * gated)).astype(jnp.bfloat16)
    return lax.dot_general(out_weight, mixed, (((0,), (0,)), ((), ())), preferred_element_type=jnp.float32)
```

```python
import functools

import jax
import jax.numpy as jnp
import ml_dtypes
import numpy as np
from jax import lax
from jax.experimental import pallas as pl
from jax.experimental.pallas import tpu as pltpu
from jax.sharding import PartitionSpec as P

MESH = pl.DeviceIdType.MESH
HALVES = 2
TILE = 256


def tables(length):
    n = np.arange(length, dtype=np.int64)[:, None]
    f = np.arange(length, dtype=np.int64)[None, :]
    angle = np.pi / (2 * length) * (((2 * f + 1) * n) % (4 * length))
    count = length // TILE
    cos = np.cos(angle).reshape(length, count, TILE)
    sin = np.sin(angle).reshape(length, count, TILE)
    both = np.concatenate([cos, sin], axis=2).transpose(1, 0, 2)
    high = both.astype(np.float32).astype(ml_dtypes.bfloat16)
    low = (both - high.astype(np.float64)).astype(np.float32).astype(ml_dtypes.bfloat16)
    return np.stack([high, low], axis=1)


def dot(a, b):
    return lax.dot_general(a, b, (((1,), (0,)), ((), ())), preferred_element_type=jnp.float32)


def dot_t(a, b):
    return lax.dot_general(a, b, (((1,), (1,)), ((), ())), preferred_element_type=jnp.float32)


def kernel(
    zs, chips,
    q_ref, k_ref, v_ref, f_ref, gain_ref, w_hbm, tab_hbm,
    out_ref,
    w_ref, tab_ref, sig_out, sig_in, acc, conv_out, conv_in, mix_hi, mix_lo,
    core_out, core_in, chip_out, chip_in,
    load_sem, sig_send, sig_recv, conv_send, conv_recv, core_send, core_recv, chip_send, chip_recv,
):
    place = lax.axis_index("seq")
    chan = lax.axis_index("chan")
    chip = chan // 2
    core = chan % 2
    other = chip * 2 + (1 - core)
    rows, width = q_ref.shape
    group = rows // zs
    half = group // HALVES
    length = zs * width
    feats = out_ref.shape[1]

    def at(c, s):
        return {"chan": c, "seq": s}

    tab_copy = pltpu.make_async_copy(tab_hbm, tab_ref, load_sem.at[0])
    tab_copy.start()
    w_copy = pltpu.make_async_copy(w_hbm, w_ref, load_sem.at[1])
    w_copy.start()

    barrier = pltpu.get_barrier_semaphore()
    for step in range(1, zs):
        pl.semaphore_signal(barrier, inc=1, device_id=at(chan, (place + step) % zs), device_id_type=MESH)
    for step in range(1, chips):
        pl.semaphore_signal(
            barrier, inc=1, device_id=at((chip + step) % chips * 2 + core, place), device_id_type=MESH
        )
    pl.semaphore_signal(barrier, inc=1, device_id=at(other, place), device_id_type=MESH)

    for j in range(zs):
        for h in range(HALVES):
            here = pl.ds(j * group + h * half, half)
            g = k_ref[here, :].astype(jnp.float32) * v_ref[here, :].astype(jnp.float32)
            sig_out[h, j, 0] = g.astype(jnp.bfloat16)
            sig_out[h, j, 1] = f_ref[here, :].astype(jnp.bfloat16)

    pl.semaphore_wait(barrier, zs + chips - 1)

    columns = pl.ds(pl.multiple_of(place * width, width), width)
    sends = []
    for h in range(HALVES):
        for step in range(1, zs):
            to = (place + step) % zs
            copy = pltpu.make_async_remote_copy(
                src_ref=sig_out.at[h, to],
                dst_ref=sig_in.at[h, :, :, columns],
                send_sem=sig_send.at[h, step],
                recv_sem=sig_recv.at[h, step],
                device_id=at(chan, to),
                device_id_type=MESH,
            )
            copy.start()
            sends.append(copy)
    for h in range(HALVES):
        sig_in[h, :, :, columns] = sig_out[h, place]

    tab_copy.wait()
    backs = []
    for h in range(HALVES):
        for step in range(1, zs):
            sends[h * (zs - 1) + step - 1].wait_recv()
        acc[...] = jnp.zeros_like(acc)

        def tile(i, carry):
            both = sig_in[h].reshape(2 * half, length)
            spec = dot(both, tab_ref[i, 0]) + dot(both, tab_ref[i, 1])
            ga, gb = spec[:half, :TILE], spec[:half, TILE:]
            fa, fb = spec[half:, :TILE], spec[half:, TILE:]
            prod = jnp.concatenate([ga * fa - gb * fb, ga * fb + gb * fa], axis=1)
            high = prod.astype(jnp.bfloat16)
            low = (prod - high.astype(jnp.float32)).astype(jnp.bfloat16)
            acc[...] += (
                dot_t(high, tab_ref[i, 0]) + dot_t(low, tab_ref[i, 0]) + dot_t(high, tab_ref[i, 1])
            )
            return carry

        lax.fori_loop(0, length // TILE, tile, 0)
        for j in range(zs):
            conv_out[h, j] = (acc[:, j * width : (j + 1) * width] * (1.0 / length)).astype(jnp.bfloat16)
        for step in range(1, zs):
            to = (place + step) % zs
            copy = pltpu.make_async_remote_copy(
                src_ref=conv_out.at[h, to],
                dst_ref=conv_in.at[place, h],
                send_sem=conv_send.at[h, step],
                recv_sem=conv_recv.at[h, step],
                device_id=at(chan, to),
                device_id_type=MESH,
            )
            copy.start()
            backs.append(copy)
        conv_in[place, h] = conv_out[h, place]

    for copy in backs:
        copy.wait_recv()
    for j in range(zs):
        for h in range(HALVES):
            start = j * group + h * half
            here = pl.ds(start, half)
            g = k_ref[here, :].astype(jnp.float32) * v_ref[here, :].astype(jnp.float32)
            total = conv_in[j, h].astype(jnp.float32) + gain_ref[here, :] * g
            mixed = (q_ref[here, :].astype(jnp.float32) * total).T
            high = mixed.astype(jnp.bfloat16)
            mix_hi[:, here] = high
            mix_lo[:, here] = (mixed - high.astype(jnp.float32)).astype(jnp.bfloat16)

    w_copy.wait()

    def part(target):
        w = w_ref[:, pl.ds(pl.multiple_of(target * feats, feats), feats)]
        return dot(mix_hi[...], w) + dot(mix_lo[...], w)

    cores = []
    for step in range(chips):
        d = (chip + 1 + step) % chips
        core_out[step] = part(d * 2 + (1 - core))
        copy = pltpu.make_async_remote_copy(
            src_ref=core_out.at[step],
            dst_ref=core_in.at[step],
            send_sem=core_send.at[step],
            recv_sem=core_recv.at[step],
            device_id=at(other, place),
            device_id_type=MESH,
        )
        copy.start()
        cores.append(copy)
    hops = []
    for step in range(chips):
        d = (chip + 1 + step) % chips
        mine = part(d * 2 + core)
        cores[step].wait_recv()
        mine = mine + core_in[step]
        if step < chips - 1:
            chip_out[step] = mine.astype(jnp.bfloat16)
            copy = pltpu.make_async_remote_copy(
                src_ref=chip_out.at[step],
                dst_ref=chip_in.at[step],
                send_sem=chip_send.at[step],
                recv_sem=chip_recv.at[step],
                device_id=at(d * 2 + core, place),
                device_id_type=MESH,
            )
            copy.start()
            hops.append(copy)
        else:
            out_ref[...] = mine
    for step in range(chips - 1):
        hops[step].wait_recv()
        out_ref[...] += chip_in[step].astype(jnp.float32)
    for copy in sends + backs + cores + hops:
        copy.wait_send()


def shards(zs, chans, queries, key_rows, value_rows, filters, skip_gain, out_weight):
    rows, width = queries.shape
    chips = chans // 2
    length = zs * width
    group = rows // zs
    half = group // HALVES
    features = out_weight.shape[1]
    feats = features // chans
    table = jnp.asarray(tables(length))
    vmem = pl.BlockSpec(memory_space=pltpu.VMEM)
    hbm = pl.BlockSpec(memory_space=pl.ANY)
    dma = pltpu.SemaphoreType.DMA
    bf16, f32 = jnp.bfloat16, jnp.float32
    out = pl.pallas_call(
        functools.partial(kernel, zs, chips),
        out_shape=jax.ShapeDtypeStruct((width, feats), f32),
        in_specs=[vmem] * 5 + [hbm] * 2,
        out_specs=vmem,
        scratch_shapes=[
            pltpu.VMEM((rows, features), bf16),
            pltpu.VMEM(table.shape, bf16),
            pltpu.VMEM((HALVES, zs, 2, half, width), bf16),
            pltpu.VMEM((HALVES, 2, half, length), bf16),
            pltpu.VMEM((half, length), f32),
            pltpu.VMEM((HALVES, zs, half, width), bf16),
            pltpu.VMEM((zs, HALVES, half, width), bf16),
            pltpu.VMEM((width, rows), bf16),
            pltpu.VMEM((width, rows), bf16),
            pltpu.VMEM((chips, width, feats), f32),
            pltpu.VMEM((chips, width, feats), f32),
            pltpu.VMEM((chips, width, feats), bf16),
            pltpu.VMEM((chips, width, feats), bf16),
            dma((2,)),
            dma((HALVES, zs)),
            dma((HALVES, zs)),
            dma((HALVES, zs)),
            dma((HALVES, zs)),
            dma((chips,)),
            dma((chips,)),
            dma((chips,)),
            dma((chips,)),
        ],
        compiler_params=pltpu.CompilerParams(
            collective_id=0, has_side_effects=True, vmem_limit_bytes=56 * 2**20
        ),
    )(queries, key_rows, value_rows, filters, skip_gain[:, None], out_weight, table)
    return out.T


def solution(mesh):
    placed = (
        P("chan", "seq"),
        P("chan", "seq"),
        P("chan", "seq"),
        P("chan", "seq"),
        P("chan"),
        P("chan", None),
    )
    return jax.shard_map(
        functools.partial(shards, mesh.shape["seq"], mesh.shape["chan"]),
        mesh=mesh,
        in_specs=placed,
        out_specs=P("chan", "seq"),
        check_vma=False,
    )
```

```python
import functools

import jax
import jax.numpy as jnp
import ml_dtypes
import numpy as np
from jax import lax
from jax.experimental import pallas as pl
from jax.experimental.pallas import tpu as pltpu
from jax.sharding import PartitionSpec as P

MESH = pl.DeviceIdType.MESH
HALVES = 2
TILE = 256


def tables(length):
    n = np.arange(length, dtype=np.int64)[:, None]
    f = np.arange(length, dtype=np.int64)[None, :]
    angle = np.pi / (2 * length) * (((2 * f + 1) * n) % (4 * length))
    count = length // TILE
    cos = np.cos(angle).reshape(length, count, TILE)
    sin = np.sin(angle).reshape(length, count, TILE)
    both = np.concatenate([cos, sin], axis=2).transpose(1, 0, 2)
    high = both.astype(np.float32).astype(ml_dtypes.bfloat16)
    low = (both - high.astype(np.float64)).astype(np.float32).astype(ml_dtypes.bfloat16)
    return np.stack([high, low], axis=1)


def dot(a, b):
    return lax.dot_general(a, b, (((1,), (0,)), ((), ())), preferred_element_type=jnp.float32)


def dot_t(a, b):
    return lax.dot_general(a, b, (((1,), (1,)), ((), ())), preferred_element_type=jnp.float32)


def kernel(
    zs, chips, halves,
    q_ref, k_ref, v_ref, f_ref, gain_ref, w_hbm, tab_hbm,
    out_ref,
    w_ref, tab_ref, sig_out, sig_in, acc, conv_out, conv_in, skip, mix_hi, mix_lo, own,
    core_out, core_in, chip_out, chip_in,
    tab_sem, w_sem, sig_send, sig_recv, conv_send, conv_recv,
    core_send, core_recv, chip_send, chip_recv,
):
    place = lax.axis_index("seq")
    chan = lax.axis_index("chan")
    chip = chan // 2
    core = chan % 2
    other = chip * 2 + (1 - core)
    rows, width = q_ref.shape
    group = rows // zs
    half = group // halves
    length = zs * width
    feats = out_ref.shape[0]
    pieces, piece = conv_out.shape[2], conv_out.shape[4]

    def at(c, s):
        return {"chan": c, "seq": s}

    barrier = pltpu.get_barrier_semaphore()
    for step in range(1, zs):
        pl.semaphore_signal(barrier, inc=1, device_id=at(chan, (place + step) % zs), device_id_type=MESH)
    for step in range(1, chips):
        pl.semaphore_signal(
            barrier, inc=1, device_id=at((chip + step) % chips * 2 + core, place), device_id_type=MESH
        )
    pl.semaphore_signal(barrier, inc=1, device_id=at(other, place), device_id_type=MESH)

    tab_copy = pltpu.make_async_copy(tab_hbm, tab_ref, tab_sem)
    tab_copy.start()
    w_copies = []
    for h in range(halves):
        for j in range(zs):
            copy = pltpu.make_async_copy(
                w_hbm.at[pl.ds(j * group + h * half, half), :],
                w_ref.at[h, pl.ds(j * half, half), :],
                w_sem.at[h, j],
            )
            copy.start()
            w_copies.append(copy)

    columns = pl.ds(pl.multiple_of(place * width, width), width)
    sends = []
    for h in range(halves):
        for j in range(zs):
            here = pl.ds(j * group + h * half, half)
            g = k_ref[here, :].astype(jnp.float32) * v_ref[here, :].astype(jnp.float32)
            sig_out[h, j, 0] = g.astype(jnp.bfloat16)
            sig_out[h, j, 1] = f_ref[here, :].astype(jnp.bfloat16)
        if h == 0:
            pl.semaphore_wait(barrier, zs + chips - 1)
        for step in range(1, zs):
            to = (place + step) % zs
            copy = pltpu.make_async_remote_copy(
                src_ref=sig_out.at[h, to],
                dst_ref=sig_in.at[h, :, :, columns],
                send_sem=sig_send.at[h, step],
                recv_sem=sig_recv.at[h, step],
                device_id=at(chan, to),
                device_id_type=MESH,
            )
            copy.start()
            sends.append(copy)
    for h in range(halves):
        sig_in[h, :, :, columns] = sig_out[h, place]

    for r in range(rows // 128):
        here = pl.ds(r * 128, 128)
        gain = jnp.broadcast_to(gain_ref[r : r + 1, :], (128, 128)).T[:, :1]
        skip[here, :] = gain * (k_ref[here, :].astype(jnp.float32) * v_ref[here, :].astype(jnp.float32))

    def part(h, target, span):
        w = w_ref[h, :, pl.ds(pl.multiple_of(target * feats, feats), feats)]
        return dot(mix_hi[h, span], w) + dot(mix_lo[h, span], w)

    def span_of(p):
        return pl.ds(p * piece, piece)

    def chip_at(step):
        return (chip + 1 + step) % chips

    def mix(h, p):
        span = span_of(p)
        for step in range(1, zs):
            backs[(h * pieces + p) * (zs - 1) + step - 1].wait_recv()
        for j in range(zs):
            here = pl.ds(j * group + h * half, half)
            total = conv_in[j, h, p].astype(jnp.float32) + skip[here, span]
            mixed = (q_ref[here, span].astype(jnp.float32) * total).T
            high = mixed.astype(jnp.bfloat16)
            mix_hi[h, span, j * half : (j + 1) * half] = high
            mix_lo[h, span, j * half : (j + 1) * half] = (mixed - high.astype(jnp.float32)).astype(jnp.bfloat16)

    def early(h):
        for p in range(pieces):
            mix(h, p)
        for step in range(chips):
            first = part(h, chip_at(step) * 2 + (1 - core), slice(None))
            second = part(h, chip_at(step) * 2 + core, slice(None))
            core_out[step] = first if h == 0 else core_out[step] + first
            own[step] = second if h == 0 else own[step] + second

    tab_copy.wait()
    for copy in w_copies:
        copy.wait()
    backs = []
    for h in range(halves):
        for step in range(1, zs):
            sends[h * (zs - 1) + step - 1].wait_recv()
        acc[...] = jnp.zeros_like(acc)

        def tile(i, carry):
            both = sig_in[h].reshape(2 * half, length)
            spec = dot(both, tab_ref[i, 0]) + dot(both, tab_ref[i, 1])
            ga, gb = spec[:half, :TILE], spec[:half, TILE:]
            fa, fb = spec[half:, :TILE], spec[half:, TILE:]
            prod = jnp.concatenate([ga * fa - gb * fb, ga * fb + gb * fa], axis=1)
            high = prod.astype(jnp.bfloat16)
            low = (prod - high.astype(jnp.float32)).astype(jnp.bfloat16)
            acc[...] += (
                dot_t(high, tab_ref[i, 0]) + dot_t(low, tab_ref[i, 0]) + dot_t(high, tab_ref[i, 1])
            )
            return carry

        lax.fori_loop(0, length // TILE, tile, 0)
        for j in range(zs):
            for p in range(pieces):
                start = j * width + p * piece
                conv_out[h, j, p] = (acc[:, start : start + piece] * (1.0 / length)).astype(jnp.bfloat16)
        for p in range(pieces):
            for step in range(1, zs):
                to = (place + step) % zs
                copy = pltpu.make_async_remote_copy(
                    src_ref=conv_out.at[h, to, p],
                    dst_ref=conv_in.at[place, h, p],
                    send_sem=conv_send.at[h, p, step],
                    recv_sem=conv_recv.at[h, p, step],
                    device_id=at(chan, to),
                    device_id_type=MESH,
                )
                copy.start()
                backs.append(copy)
        conv_in[place, h] = conv_out[h, place]
        if h == halves - 1:
            for early_h in range(halves - 1):
                early(early_h)

    last = halves - 1
    cores, hops = [], []

    def to_core(p, step):
        span = span_of(p)
        core_out[step, span] += part(last, chip_at(step) * 2 + (1 - core), span)
        copy = pltpu.make_async_remote_copy(
            src_ref=core_out.at[step, span],
            dst_ref=core_in.at[step, span],
            send_sem=core_send.at[p, step],
            recv_sem=core_recv.at[p, step],
            device_id=at(other, place),
            device_id_type=MESH,
        )
        copy.start()
        cores.append(copy)

    def to_chip(p, step):
        span = span_of(p)
        mine = own[step, span] + part(last, chip_at(step) * 2 + core, span)
        cores[p * chips + step].wait_recv()
        mine = (mine + core_in[step, span]).T
        if step == chips - 1:
            out_ref[:, span] = mine
            return
        chip_out[p, step] = mine.astype(jnp.bfloat16)
        copy = pltpu.make_async_remote_copy(
            src_ref=chip_out.at[p, step],
            dst_ref=chip_in.at[p, step],
            send_sem=chip_send.at[p, step],
            recv_sem=chip_recv.at[p, step],
            device_id=at(chip_at(step) * 2 + core, place),
            device_id_type=MESH,
        )
        copy.start()
        hops.append(copy)

    for p in range(pieces):
        mix(last, p)
        to_core(p, 0)
        for step in range(1, chips):
            to_core(p, step)
            to_chip(p, step - 1)
        to_chip(p, chips - 1)
    for p in range(pieces):
        for step in range(chips - 1):
            hops[p * (chips - 1) + step].wait_recv()
            out_ref[:, span_of(p)] += chip_in[p, step].astype(jnp.float32)
    for copy in sends + backs + cores + hops:
        copy.wait_send()


def shards(zs, chans, queries, key_rows, value_rows, filters, skip_gain, out_weight):
    rows, width = queries.shape
    chips = chans // 2
    length = zs * width
    group = rows // zs
    halves = HALVES if group % (16 * HALVES) == 0 else 1
    half = group // halves
    pieces = 2 if width % 256 == 0 else 1
    piece = width // pieces
    features = out_weight.shape[1]
    feats = features // chans
    table = jnp.asarray(tables(length))
    vmem = pl.BlockSpec(memory_space=pltpu.VMEM)
    hbm = pl.BlockSpec(memory_space=pl.ANY)
    dma = pltpu.SemaphoreType.DMA
    bf16, f32 = jnp.bfloat16, jnp.float32
    out = pl.pallas_call(
        functools.partial(kernel, zs, chips, halves),
        out_shape=jax.ShapeDtypeStruct((feats, width), f32),
        in_specs=[vmem] * 5 + [hbm] * 2,
        out_specs=vmem,
        scratch_shapes=[
            pltpu.VMEM((halves, zs * half, features), bf16),
            pltpu.VMEM(table.shape, bf16),
            pltpu.VMEM((halves, zs, 2, half, width), bf16),
            pltpu.VMEM((halves, 2, half, length), bf16),
            pltpu.VMEM((half, length), f32),
            pltpu.VMEM((halves, zs, pieces, half, piece), bf16),
            pltpu.VMEM((zs, halves, pieces, half, piece), bf16),
            pltpu.VMEM((rows, width), f32),
            pltpu.VMEM((halves, width, zs * half), bf16),
            pltpu.VMEM((halves, width, zs * half), bf16),
            pltpu.VMEM((chips, width, feats), f32),
            pltpu.VMEM((chips, width, feats), f32),
            pltpu.VMEM((chips, width, feats), f32),
            pltpu.VMEM((pieces, chips, feats, piece), bf16),
            pltpu.VMEM((pieces, chips, feats, piece), bf16),
            dma,
            dma((halves, zs)),
            dma((halves, zs)),
            dma((halves, zs)),
            dma((halves, pieces, zs)),
            dma((halves, pieces, zs)),
            dma((pieces, chips)),
            dma((pieces, chips)),
            dma((pieces, chips)),
            dma((pieces, chips)),
        ],
        compiler_params=pltpu.CompilerParams(
            collective_id=0, has_side_effects=True, vmem_limit_bytes=56 * 2**20
        ),
    )(queries, key_rows, value_rows, filters, skip_gain.reshape(-1, 128), out_weight, table)
    return out


def solution(mesh):
    placed = (
        P("chan", "seq"),
        P("chan", "seq"),
        P("chan", "seq"),
        P("chan", "seq"),
        P("chan"),
        P("chan", None),
    )
    return jax.shard_map(
        functools.partial(shards, mesh.shape["seq"], mesh.shape["chan"]),
        mesh=mesh,
        in_specs=placed,
        out_specs=P("chan", "seq"),
        check_vma=False,
    )
```
